32 devices in a mesh: dp: 8 (over z, x), work: 4 (over y, core).
Axes of the slice: x: 2, y: 2, z: 4, core: 2. Of those that a mesh axis runs over, the one named last changes fastest.
Arguments:
- act_one: bfloat16 [1024, 5120], P('dp', 'work')
- grad_one: bfloat16 [1024, 5120], P('dp', 'work')
- act_two: bfloat16 [1024, 5120], P('dp', 'work')
- grad_two: bfloat16 [1024, 5120], P('dp', 'work')
- owner_table: int32 [4, 6], replicated, may hold values from -1 to 79, as said below
Outputs:
- eigen_blocks: float32 [4, 6, 256, 256], replicated
The draws below stay inside these ranges and needn't reach their ends.
Inputs may be any that keep to these rules, and one draw needn't show every extreme that they name: `owner_table`: an entry names factor block f * 20 + k (block k of input f) or is -1 for an empty slot. Exactly 12 slots are filled, no block appears twice, and at least one owner has all 6 slots filled. Block k's features lie on work member (k mod (20)) // (5120 / (256 * 4)); no member holds more than 6 filled blocks, and one member holds exactly 6.
All inputs are finite; a program needn't handle non-finite values.
Results may differ from the reference program's by a relative error of at most 0.0003.
Values sent between devices are 32-bit elements; how exact they have to be, the bound alone decides.
A program may use at most 64 MiB of HBM per device.

```python
import math
from functools import partial
import jax
import jax.numpy as jnp
from jax import lax

D = 5120
BS = 256
SLOTS = 6
ITERS = 4
TOKENS = 1024
N_WORK = 4


def feature_law(key, common_size, row_span):
    subkeys = jax.random.split(key, 6)
    normal_part = jax.random.normal(subkeys[0], (TOKENS, D), jnp.float32)
    jitter = normal_part
    column_scale = jnp.exp(jax.random.uniform(subkeys[2], (1, D), jnp.float32, -0.7, 0.7))
    features = jitter * column_scale
    latents = jax.random.normal(subkeys[3], (TOKENS, 4), jnp.float32)
    loadings = common_size * jax.random.normal(subkeys[4], (4, D), jnp.float32)
    for index in range(4):
        features = features + latents[:, index:index + 1] * loadings[index:index + 1, :]
    position = jnp.arange(TOKENS, dtype=jnp.float32)[:, None] / TOKENS
    roughness = jax.random.uniform(subkeys[5], (TOKENS, 1), jnp.float32, 0.6, 1.4)
    row_scale = jnp.exp(row_span * (position - 0.5)) * roughness
    return (features * row_scale).astype(jnp.bfloat16)


def draw_act_one(key, part):
    key = jax.random.fold_in(key, 11)
    return feature_law(key, 0.2, math.log(3.0))


def draw_grad_one(key, part):
    key = jax.random.fold_in(key, 12)
    return feature_law(key, 0.2, math.log(3.0))


def draw_act_two(key, part):
    key = jax.random.fold_in(key, 13)
    return feature_law(key, 0.2, math.log(3.0))


def draw_grad_two(key, part):
    key = jax.random.fold_in(key, 14)
    return feature_law(key, 0.2, math.log(3.0))


def draw_owner_table(key, part):
    key = jax.random.fold_in(key, 29)
    subkeys = jax.random.split(key, 6)
    filled_count = N_WORK * SLOTS // 2
    spare_count = filled_count - SLOTS
    busiest = jax.random.randint(subkeys[0], (), 0, N_WORK)
    shuffled = jax.random.permutation(subkeys[1], (N_WORK - 1) * SLOTS)
    others_filled = shuffled < spare_count
    row_ids = jnp.arange(N_WORK, dtype=jnp.int32)[:, None]
    col_ids = jnp.arange(SLOTS, dtype=jnp.int32)[None, :]
    other_row = row_ids - (row_ids > busiest).astype(jnp.int32)
    position = jnp.clip(other_row * SLOTS + col_ids, 0, (N_WORK - 1) * SLOTS - 1)
    filled = jnp.where(row_ids == busiest, True, others_filled[position]).reshape(-1)
    ranking = jnp.clip(jnp.cumsum(filled.astype(jnp.int32)) - 1, 0, filled_count - 1)
    per_holder = D // (BS * N_WORK)
    per_factor = D // BS
    held_total = 4 * per_holder
    heavy = jax.random.randint(subkeys[2], (), 0, N_WORK)
    sequence = jnp.arange(filled_count, dtype=jnp.int32)
    later = jnp.clip(sequence - SLOTS, 0, None)
    other_pick = later % (N_WORK - 1)
    other_holder = other_pick + (other_pick >= heavy).astype(jnp.int32)
    holder_seq = jnp.where(sequence < SLOTS, heavy, other_holder)
    occurrence = jnp.where(sequence < SLOTS, sequence, later // (N_WORK - 1))
    holder_keys = jax.random.split(subkeys[3], N_WORK)
    drawn_perms = jax.vmap(lambda sub: jax.random.permutation(sub, held_total))(holder_keys)
    rest_perm = jax.random.permutation(subkeys[4], held_total - 1)
    top_perm = jnp.concatenate([jnp.array([held_total - 1], jnp.int32), rest_perm.astype(jnp.int32)])
    perms = jnp.where((jnp.arange(N_WORK, dtype=jnp.int32) == N_WORK - 1)[:, None], top_perm[None, :], drawn_perms.astype(jnp.int32))
    local_pick = perms[holder_seq, occurrence]
    block_seq = local_pick // per_holder * per_factor + holder_seq * per_holder + local_pick % per_holder
    rank_perm = jax.random.permutation(subkeys[5], filled_count)
    top_index = jnp.argmax((holder_seq == N_WORK - 1) & (occurrence == 0)).astype(jnp.int32)
    rank_perm = jnp.where(rank_perm == top_index, rank_perm[0], rank_perm)
    rank_perm = rank_perm.at[0].set(top_index)
    chosen = block_seq[rank_perm[ranking]]
    return jnp.where(filled, chosen, -1).reshape(N_WORK, SLOTS).astype(jnp.int32)


def setup_inputs(seed: int = 0) -> dict:
    keys = jax.random.split(jax.random.key(seed), 6)
    act_one = draw_act_one(jax.random.fold_in(keys[5], 71), 0)
    grad_one = draw_grad_one(jax.random.fold_in(keys[5], 71), 0)
    act_two = draw_act_two(jax.random.fold_in(keys[5], 71), 0)
    grad_two = draw_grad_two(jax.random.fold_in(keys[5], 71), 0)
    owner_table = draw_owner_table(jax.random.fold_in(keys[5], 71), 0)
    return dict(act_one=act_one, grad_one=grad_one, act_two=act_two, grad_two=grad_two, owner_table=owner_table)


DAMPING = 0.1

def block_factor(features, first_col):
    column_block = lax.dynamic_slice_in_dim(features, first_col, BS, 1)
    inner_gram = jnp.dot(column_block.T.astype(jnp.float32), column_block.astype(jnp.float32), preferred_element_type=jnp.float32) / TOKENS
    mean_diag = jnp.trace(inner_gram) / BS
    return inner_gram + DAMPING * mean_diag * jnp.eye(BS, dtype=jnp.float32)

def orthogonal_steps(factor):
    eigen_basis = jnp.broadcast_to(jnp.eye(factor.shape[-1], dtype=jnp.float32), factor.shape)
    for iteration in range(ITERS):
        projected = jnp.matmul(factor, eigen_basis, precision=lax.Precision.HIGHEST)
        inner_gram = jnp.matmul(jnp.swapaxes(projected, -1, -2), projected, precision=lax.Precision.HIGHEST)
        lower_factor = lax.linalg.cholesky(inner_gram)
        eigen_basis = lax.linalg.triangular_solve(lower_factor, projected, left_side=False, lower=True, transpose_a=True)
    return eigen_basis

def reference(act_one, grad_one, act_two, grad_two, owner_table):
    per_factor = D // BS
    factor_inputs = (act_one, grad_one, act_two, grad_two)
    branches = [partial(block_factor, source) for source in factor_inputs]

    def one_slot(table_entry):
        block_id = jnp.maximum(table_entry, 0)
        factor_id = block_id // per_factor
        first_col = (block_id % per_factor * BS).astype(jnp.int32)
        factor = lax.switch(factor_id, branches, first_col)
        eigen_basis = orthogonal_steps(factor) * math.sqrt(BS)
        return jnp.where(table_entry >= 0, eigen_basis, jnp.zeros_like(eigen_basis))
    refreshed = lax.map(one_slot, owner_table.reshape(-1))
    return refreshed.reshape(N_WORK, SLOTS, BS, BS)
```

```python
import functools
import math

import jax
import jax.numpy as jnp
from jax import lax
from jax.experimental import pallas as pl
from jax.experimental.pallas import tpu as pltpu
from jax.sharding import PartitionSpec as P

BS = 256
HB = 128
ITERS = 4
DAMPING = 0.1
HI = lax.Precision.HIGHEST


def dot(a, b, ca, cb, precision=HI):
    return lax.dot_general(
        a, b, (((ca,), (cb,)), ((), ())), precision=precision, preferred_element_type=jnp.float32
    )


def inv_chol(s):
    n=HB
    row=lax.broadcasted_iota(jnp.int32,(n,n),0); col=lax.broadcasted_iota(jnp.int32,(n,n),1)
    eye=row==col
    diag=jnp.where(eye,s,0.0)
    drow=lax.rsqrt(jnp.sum(diag,axis=0,keepdims=True)); dcol=lax.rsqrt(jnp.sum(diag,axis=1,keepdims=True))
    s=s*drow*dcol
    w=[s[8*g:8*g+8,:] for g in range(n//8)]
    lane=lax.broadcasted_iota(jnp.int32,(8,n),1); sub=lax.broadcasted_iota(jnp.int32,(8,n),0)
    for j in range(n):
        g0,t=divmod(j,8)
        r=jnp.broadcast_to(w[g0][t:t+1,:],(8,n))
        p=jnp.broadcast_to(r[:,j:j+1],(8,n))
        inv=1.0/p
        rr=jnp.where(lane==j,1.0+inv,r*inv)
        for g in range(g0,n//8):
            if g==g0 and t==7: continue
            c=jnp.broadcast_to(w[g][:,j:j+1],(8,n))
            if g==g0: c=jnp.where(sub>t,c,0.0)
            w[g]=w[g]-c*rr
    w=jnp.concatenate(w,axis=0)
    d=lax.rsqrt(jnp.sum(jnp.where(eye,w,0.0),axis=1,keepdims=True))
    return jnp.where(col<row,w,jnp.where(eye,1.0,0.0))*d*drow

def basis_body(x_ref,tokens,f_ref,y_ref,q_ref):
    x=x_ref[...].astype(jnp.bfloat16)
    g=lax.dot_general(x,x,(((0,),(0,)),((),())),preferred_element_type=jnp.float32)*(1.0/tokens)
    row=lax.broadcasted_iota(jnp.int32,(BS,BS),0); col=lax.broadcasted_iota(jnp.int32,(BS,BS),1)
    eye=row==col
    tr=jnp.sum(jnp.sum(jnp.where(eye,g,0.0),axis=0,keepdims=True),axis=1,keepdims=True)/BS
    f=g+jnp.where(eye,DAMPING*tr,0.0)
    f_ref[...]=f
    y_ref[...]=f
    def it(i,_):
        y1=y_ref[:,:HB]
        b1=inv_chol(dot(y1,y1,0,0))
        q1=dot(y1,b1,1,1)
        q_ref[:,:HB]=q1
        y2=y_ref[:,HB:]
        z2=y2-dot(q1,dot(q1,y2,0,0),1,0)
        b2=inv_chol(dot(z2,z2,0,0))
        q_ref[:,HB:]=dot(z2,b2,1,1)
        @pl.when(i<ITERS-1)
        def _():
            y_ref[...]=dot(f_ref[...],q_ref[...],1,0)
        return 0
    lax.fori_loop(0,ITERS,it,0)


def pick_kernel(per_holder, per_factor, slots, table_ref, *refs):
    sources, out_ref, held, sems = refs[:4], refs[4], refs[5], refs[6]
    member = lax.axis_index("work")
    owners, per_owner = table_ref.shape

    def locate(i):
        b = table_ref[i // per_owner, i % per_owner]
        within = b % per_factor
        mine = (b >= 0) & (within // per_holder == member)
        return b // per_factor, within % per_holder, mine

    def begin(i, count):
        source, k, mine = locate(i)
        for f in range(4):

            @pl.when(mine & (source == f))
            def _():
                cols = pl.ds(pl.multiple_of(k * BS, BS), BS)
                slot = jnp.minimum(count, slots - 1)
                pltpu.make_async_copy(sources[f].at[:, cols], held.at[slot], sems.at[slot]).start()

        return count + jnp.where(mine, 1, 0)

    count = lax.fori_loop(0, owners * per_owner, begin, 0)
    for j in range(out_ref.shape[0]):
        if j >= slots:
            out_ref[j] = jnp.zeros(out_ref.shape[1:], jnp.float32)
            continue

        @pl.when(j < count)
        def _():
            pltpu.make_async_copy(sources[0].at[:, pl.ds(0, BS)], held.at[j], sems.at[j]).wait()
            out_ref[j] = held[j].astype(jnp.float32)

        @pl.when(j >= count)
        def _():
            out_ref[j] = jnp.zeros(out_ref.shape[1:], jnp.float32)


def pick(table, sources, per_holder, per_factor, slots, places):
    rows = sources[0].shape[0]
    return pl.pallas_call(
        functools.partial(pick_kernel, per_holder, per_factor, slots),
        out_shape=jax.ShapeDtypeStruct((places, rows, BS), jnp.float32),
        in_specs=[pl.BlockSpec(memory_space=pltpu.SMEM)] + [pl.BlockSpec(memory_space=pl.ANY)] * 4,
        out_specs=pl.BlockSpec(memory_space=pltpu.VMEM),
        scratch_shapes=[
            pltpu.VMEM((slots, rows, BS), jnp.bfloat16),
            pltpu.SemaphoreType.DMA((slots,)),
        ],
        compiler_params=pltpu.CompilerParams(vmem_limit_bytes=48 << 20),
    )(table, *sources)


def place_kernel(per_holder, per_factor, workers, table_ref, bases_ref, out_ref, zeros, counts, sems):
    owners, per_owner = table_ref.shape
    zeros[...] = jnp.zeros_like(zeros)
    for h in range(workers):
        counts[h] = 0

    def begin(i, carry):
        b = table_ref[i // per_owner, i % per_owner]

        @pl.when(b >= 0)
        def _():
            holder = b % per_factor // per_holder
            nth = counts[holder]
            counts[holder] = nth + 1
            pltpu.make_async_copy(
                bases_ref.at[nth * workers + holder], out_ref.at[i], sems.at[i]
            ).start()

        @pl.when(b < 0)
        def _():
            pltpu.make_async_copy(zeros, out_ref.at[i], sems.at[i]).start()

        return carry

    lax.fori_loop(0, owners * per_owner, begin, 0)

    def end(i, carry):
        pltpu.make_async_copy(zeros, out_ref.at[i], sems.at[i]).wait()
        return carry

    lax.fori_loop(0, owners * per_owner, end, 0)


def place(table, bases, per_holder, per_factor, workers):
    flat = table.shape[0] * table.shape[1]
    return pl.pallas_call(
        functools.partial(place_kernel, per_holder, per_factor, workers),
        out_shape=jax.ShapeDtypeStruct((flat, BS, BS), jnp.float32),
        in_specs=[pl.BlockSpec(memory_space=pltpu.SMEM), pl.BlockSpec(memory_space=pl.ANY)],
        out_specs=pl.BlockSpec(memory_space=pl.ANY),
        scratch_shapes=[
            pltpu.VMEM((BS, BS), jnp.float32),
            pltpu.SMEM((workers,), jnp.int32),
            pltpu.SemaphoreType.DMA((flat,)),
        ],
    )(table, bases)


def basis_kernel(x_ref, o_ref, f_ref, y_ref):
    basis_body(x_ref, x_ref.shape[0], f_ref, y_ref, o_ref)
    o_ref[...] = o_ref[...] * math.sqrt(BS)


def basis(x):
    return pl.pallas_call(
        basis_kernel,
        out_shape=jax.ShapeDtypeStruct((BS, BS), jnp.float32),
        scratch_shapes=[pltpu.VMEM((BS, BS), jnp.float32)] * 2,
        compiler_params=pltpu.CompilerParams(vmem_limit_bytes=48 << 20),
    )(x)


def per_device(act_one, grad_one, act_two, grad_two, owner_table):
    workers = lax.axis_size("work")
    replicas = lax.axis_size("dp")
    tok_rows, feature_width = act_one.shape
    per_holder = feature_width // BS
    per_factor = per_holder * workers
    slots = owner_table.shape[1]
    span = next(n for n in range(slots, replicas + 1) if replicas % n == 0)
    picked = pick(
        owner_table, (act_one, grad_one, act_two, grad_two), per_holder, per_factor, slots, span
    )
    picked = jnp.tile(picked, (replicas // span, 1, 1))
    mine = lax.all_to_all(picked, "dp", split_axis=0, concat_axis=0, tiled=True)
    base = basis(mine.reshape(replicas * tok_rows, BS))
    groups = None
    if span < replicas:
        each = span * workers
        groups = [list(range(i, i + each)) for i in range(0, replicas * workers, each)]
    bases = lax.all_gather(base, ("dp", "work"), axis=0, tiled=False, axis_index_groups=groups)
    placed = place(owner_table, bases, per_holder, per_factor, workers)
    return placed.reshape(workers, slots, BS, BS)


def solution(mesh):
    in_specs = (P("dp", "work"), P("dp", "work"), P("dp", "work"), P("dp", "work"), P())
    return jax.shard_map(
        per_device, mesh=mesh, in_specs=in_specs, out_specs=P(), check_vma=False
    )
```

```python
import functools
import math

import jax
import jax.numpy as jnp
from jax import lax
from jax.experimental import pallas as pl
from jax.experimental.pallas import tpu as pltpu
from jax.sharding import PartitionSpec as P

BS = 256
NB = 32
ITERS = 4
DAMPING = 0.1
HI = lax.Precision.HIGHEST


def dot(a, b, ca, cb, precision=HI):
    return lax.dot_general(
        a, b, (((ca,), (cb,)), ((), ())), precision=precision, preferred_element_type=jnp.float32
    )


def eliminate(mats, n):
    row = lax.broadcasted_iota(jnp.int32, (n, n), 0)
    col = lax.broadcasted_iota(jnp.int32, (n, n), 1)
    eye = row == col
    lane = lax.broadcasted_iota(jnp.int32, (8, n), 1)
    sub = lax.broadcasted_iota(jnp.int32, (8, n), 0)
    scales, works = [], []
    for s in mats:
        diag = jnp.where(eye, s, 0.0)
        down = lax.rsqrt(jnp.sum(diag, axis=0, keepdims=True))
        across = lax.rsqrt(jnp.sum(diag, axis=1, keepdims=True))
        s = s * down * across
        scales.append(down)
        works.append([s[8 * g : 8 * g + 8, :] for g in range(n // 8)])
    for j in range(n):
        first, t = divmod(j, 8)
        for w in works:
            pivot = jnp.broadcast_to(w[first][:, j : j + 1], (8, n))
            inverse = 1.0 / pivot
            scaled = jnp.where(lane == j, 1.0 + inverse, w[first] * inverse)
            scaled = jnp.broadcast_to(scaled[t : t + 1, :], (8, n))
            for g in range(first, n // 8):
                if g == first:
                    if t < 7:
                        w[g] = w[g] - jnp.where(sub > t, pivot, 0.0) * scaled
                else:
                    w[g] = w[g] - jnp.broadcast_to(w[g][:, j : j + 1], (8, n)) * scaled
    found = []
    for w, down in zip(works, scales):
        w = jnp.concatenate(w, axis=0)
        d = lax.rsqrt(jnp.sum(jnp.where(eye, w, 0.0), axis=1, keepdims=True))
        found.append(jnp.where(col < row, w, jnp.where(eye, 1.0, 0.0)) * d * down)
    return found


def basis_body(x_ref, f_ref, q_ref):
    x = x_ref[...].astype(jnp.bfloat16)
    g = lax.dot_general(x, x, (((0,), (0,)), ((), ())), preferred_element_type=jnp.float32)
    g = g * (1.0 / x_ref.shape[0])
    row = lax.broadcasted_iota(jnp.int32, (BS, BS), 0)
    col = lax.broadcasted_iota(jnp.int32, (BS, BS), 1)
    eye = row == col
    trace = jnp.sum(
        jnp.sum(jnp.where(eye, g, 0.0), axis=0, keepdims=True), axis=1, keepdims=True
    )
    f_ref[...] = g + jnp.where(eye, DAMPING / BS * trace, 0.0)
    for stage in range(ITERS + BS // NB - 1):
        active = [(k, stage - k) for k in range(ITERS) if 0 <= stage - k < BS // NB]
        span = {b: slice(b * NB, b * NB + NB) for _, b in active}
        later = [(k, b) for k, b in active if k > 0]
        moved = {}
        if later:
            held = [q_ref[k - 1, span[b], :] for k, b in later]
            held = jnp.concatenate(held, axis=0) if len(held) > 1 else held[0]
            product = dot(held, f_ref[...], 1, 0)
            moved = {kb: product[i * NB : i * NB + NB] for i, kb in enumerate(later)}
        rests = []
        for k, b in active:
            y = moved[(k, b)] if k else f_ref[span[b], :]
            if b:
                before = q_ref[k, : b * NB, :]
                y = y - dot(dot(y, before, 1, 1), before, 1, 0)
            rests.append(y)
        factors = eliminate([dot(z, z, 1, 1) for z in rests], NB)
        for (k, b), z, t in zip(active, rests, factors):
            q_ref[k, span[b], :] = dot(t, z, 1, 0)


def pick_kernel(per_holder, per_factor, slots, table_ref, *refs):
    sources, out_ref, held, sems = refs[:4], refs[4], refs[5], refs[6]
    member = lax.axis_index("work")
    owners, per_owner = table_ref.shape

    def locate(i):
        b = table_ref[i // per_owner, i % per_owner]
        within = b % per_factor
        mine = (b >= 0) & (within // per_holder == member)
        return b // per_factor, within % per_holder, mine

    def begin(i, count):
        source, k, mine = locate(i)
        for f in range(4):

            @pl.when(mine & (source == f))
            def _():
                cols = pl.ds(pl.multiple_of(k * BS, BS), BS)
                slot = jnp.minimum(count, slots - 1)
                pltpu.make_async_copy(sources[f].at[:, cols], held.at[slot], sems.at[slot]).start()

        return count + jnp.where(mine, 1, 0)

    count = lax.fori_loop(0, owners * per_owner, begin, 0)
    for j in range(out_ref.shape[0]):
        if j >= slots:
            out_ref[j] = jnp.zeros(out_ref.shape[1:], jnp.float32)
            continue

        @pl.when(j < count)
        def _():
            pltpu.make_async_copy(sources[0].at[:, pl.ds(0, BS)], held.at[j], sems.at[j]).wait()
            out_ref[j] = held[j].astype(jnp.float32)

        @pl.when(j >= count)
        def _():
            out_ref[j] = jnp.zeros(out_ref.shape[1:], jnp.float32)


def pick(table, sources, per_holder, per_factor, slots, places):
    rows = sources[0].shape[0]
    return pl.pallas_call(
        functools.partial(pick_kernel, per_holder, per_factor, slots),
        out_shape=jax.ShapeDtypeStruct((places, rows, BS), jnp.float32),
        in_specs=[pl.BlockSpec(memory_space=pltpu.SMEM)] + [pl.BlockSpec(memory_space=pl.ANY)] * 4,
        out_specs=pl.BlockSpec(memory_space=pltpu.VMEM),
        scratch_shapes=[
            pltpu.VMEM((slots, rows, BS), jnp.bfloat16),
            pltpu.SemaphoreType.DMA((slots,)),
        ],
        compiler_params=pltpu.CompilerParams(vmem_limit_bytes=48 << 20),
    )(table, *sources)


def place_kernel(per_holder, per_factor, workers, table_ref, bases_ref, out_ref, held, zeros, counts, sems):
    owners, per_owner = table_ref.shape
    flat = owners * per_owner
    for h in range(workers):
        counts[h] = 0

    def begin(i, carry):
        b = table_ref[i // per_owner, i % per_owner]

        @pl.when(b >= 0)
        def _():
            holder = b % per_factor // per_holder
            nth = counts[holder]
            counts[holder] = nth + 1
            pltpu.make_async_copy(
                bases_ref.at[nth * workers + holder], held.at[i], sems.at[0, i]
            ).start()

        return carry

    lax.fori_loop(0, flat, begin, 0)
    zeros[...] = jnp.zeros_like(zeros)

    def empty(i, carry):
        @pl.when(table_ref[i // per_owner, i % per_owner] < 0)
        def _():
            pltpu.make_async_copy(zeros, out_ref.at[i], sems.at[1, i]).start()

        return carry

    lax.fori_loop(0, flat, empty, 0)

    def forward(i, carry):
        @pl.when(table_ref[i // per_owner, i % per_owner] >= 0)
        def _():
            pltpu.make_async_copy(bases_ref.at[0], held.at[i], sems.at[0, i]).wait()
            pltpu.make_async_copy(held.at[i], out_ref.at[i], sems.at[1, i]).start()

        return carry

    lax.fori_loop(0, flat, forward, 0)

    def end(i, carry):
        pltpu.make_async_copy(zeros, out_ref.at[i], sems.at[1, i]).wait()
        return carry

    lax.fori_loop(0, flat, end, 0)


def place(table, bases, per_holder, per_factor, workers):
    flat = table.shape[0] * table.shape[1]
    return pl.pallas_call(
        functools.partial(place_kernel, per_holder, per_factor, workers),
        out_shape=jax.ShapeDtypeStruct((flat, BS, BS), jnp.float32),
        in_specs=[pl.BlockSpec(memory_space=pltpu.SMEM), pl.BlockSpec(memory_space=pl.ANY)],
        out_specs=pl.BlockSpec(memory_space=pl.ANY),
        scratch_shapes=[
            pltpu.VMEM((flat, BS, BS), jnp.float32),
            pltpu.VMEM((BS, BS), jnp.float32),
            pltpu.SMEM((workers,), jnp.int32),
            pltpu.SemaphoreType.DMA((2, flat)),
        ],
        compiler_params=pltpu.CompilerParams(vmem_limit_bytes=48 << 20),
    )(table, bases)


def basis_kernel(x_ref, o_ref, f_ref, q_ref):
    basis_body(x_ref, f_ref, q_ref)
    o_ref[...] = q_ref[ITERS - 1].T * math.sqrt(BS)


def basis(x):
    return pl.pallas_call(
        basis_kernel,
        out_shape=jax.ShapeDtypeStruct((BS, BS), jnp.float32),
        scratch_shapes=[
            pltpu.VMEM((BS, BS), jnp.float32),
            pltpu.VMEM((ITERS, BS, BS), jnp.float32),
        ],
        compiler_params=pltpu.CompilerParams(vmem_limit_bytes=48 << 20),
    )(x)


def per_device(act_one, grad_one, act_two, grad_two, owner_table):
    workers = lax.axis_size("work")
    replicas = lax.axis_size("dp")
    tok_rows, feature_width = act_one.shape
    per_holder = feature_width // BS
    per_factor = per_holder * workers
    slots = owner_table.shape[1]
    span = next(n for n in range(slots, replicas + 1) if replicas % n == 0)
    picked = pick(
        owner_table, (act_one, grad_one, act_two, grad_two), per_holder, per_factor, slots, span
    )
    picked = jnp.tile(picked, (replicas // span, 1, 1))
    mine = lax.all_to_all(picked, "dp", split_axis=0, concat_axis=0, tiled=True)
    base = basis(mine.reshape(replicas * tok_rows, BS))
    groups = None
    if span < replicas:
        each = span * workers
        groups = [list(range(i, i + each)) for i in range(0, replicas * workers, each)]
    bases = lax.all_gather(base, ("dp", "work"), axis=0, tiled=False, axis_index_groups=groups)
    placed = place(owner_table, bases, per_holder, per_factor, workers)
    return placed.reshape(workers, slots, BS, BS)


def solution(mesh):
    in_specs = (P("dp", "work"), P("dp", "work"), P("dp", "work"), P("dp", "work"), P())
    return jax.shard_map(
        per_device, mesh=mesh, in_specs=in_specs, out_specs=P(), check_vma=False
    )
```

```python
import functools
import math

import jax
import jax.numpy as jnp
from jax import lax
from jax.experimental import pallas as pl
from jax.experimental.pallas import tpu as pltpu
from jax.sharding import PartitionSpec as P

BS = 256
NB = 32
ITERS = 4
DAMPING = 0.1
HI = lax.Precision.HIGHEST


def dot(a, b, ca, cb, precision=HI):
    return lax.dot_general(
        a, b, (((ca,), (cb,)), ((), ())), precision=precision, preferred_element_type=jnp.float32
    )


def eliminate(mats, n):
    row = lax.broadcasted_iota(jnp.int32, (n, n), 0)
    col = lax.broadcasted_iota(jnp.int32, (n, n), 1)
    eye = row == col
    lane = lax.broadcasted_iota(jnp.int32, (8, n), 1)
    sub = lax.broadcasted_iota(jnp.int32, (8, n), 0)
    scales, works = [], []
    for s in mats:
        diag = jnp.where(eye, s, 0.0)
        down = lax.rsqrt(jnp.sum(diag, axis=0, keepdims=True))
        across = lax.rsqrt(jnp.sum(diag, axis=1, keepdims=True))
        s = s * down * across
        scales.append(down)
        works.append([s[8 * g : 8 * g + 8, :] for g in range(n // 8)])
    for j in range(n):
        first, t = divmod(j, 8)
        for w in works:
            pivot = jnp.broadcast_to(w[first][:, j : j + 1], (8, n))
            inverse = 1.0 / pivot
            scaled = jnp.where(lane == j, 1.0 + inverse, w[first] * inverse)
            scaled = jnp.broadcast_to(scaled[t : t + 1, :], (8, n))
            for g in range(first, n // 8):
                if g == first:
                    if t < 7:
                        w[g] = w[g] - jnp.where(sub > t, pivot, 0.0) * scaled
                else:
                    w[g] = w[g] - jnp.broadcast_to(w[g][:, j : j + 1], (8, n)) * scaled
    found = []
    for w, down in zip(works, scales):
        w = jnp.concatenate(w, axis=0)
        d = lax.rsqrt(jnp.sum(jnp.where(eye, w, 0.0), axis=1, keepdims=True))
        found.append(jnp.where(col < row, w, jnp.where(eye, 1.0, 0.0)) * d * down)
    return found


def basis_body(x_ref, f_ref, q_ref):
    x = x_ref[...].astype(jnp.bfloat16)
    g = lax.dot_general(x, x, (((0,), (0,)), ((), ())), preferred_element_type=jnp.float32)
    g = g * (1.0 / x_ref.shape[0])
    row = lax.broadcasted_iota(jnp.int32, (BS, BS), 0)
    col = lax.broadcasted_iota(jnp.int32, (BS, BS), 1)
    eye = row == col
    trace = jnp.sum(
        jnp.sum(jnp.where(eye, g, 0.0), axis=0, keepdims=True), axis=1, keepdims=True
    )
    f_ref[...] = g + jnp.where(eye, DAMPING / BS * trace, 0.0)
    for stage in range(ITERS + BS // NB - 1):
        active = [(k, stage - k) for k in range(ITERS) if 0 <= stage - k < BS // NB]
        span = {b: slice(b * NB, b * NB + NB) for _, b in active}
        later = [(k, b) for k, b in active if k > 0]
        moved = {}
        if later:
            held = [q_ref[k - 1, span[b], :] for k, b in later]
            held = jnp.concatenate(held, axis=0) if len(held) > 1 else held[0]
            product = dot(held, f_ref[...], 1, 0)
            moved = {kb: product[i * NB : i * NB + NB] for i, kb in enumerate(later)}
        rests = []
        for k, b in active:
            y = moved[(k, b)] if k else f_ref[span[b], :]
            if b:
                before = q_ref[k, : b * NB, :]
                y = y - dot(dot(y, before, 1, 1), before, 1, 0)
            rests.append(y)
        factors = eliminate([dot(z, z, 1, 1) for z in rests], NB)
        for (k, b), z, t in zip(active, rests, factors):
            q_ref[k, span[b], :] = dot(t, z, 1, 0)


def pick_kernel(per_holder, per_factor, slots, table_ref, *refs):
    sources, out_ref, held, sems = refs[:4], refs[4], refs[5], refs[6]
    member = lax.axis_index("work")
    owners, per_owner = table_ref.shape

    def locate(i):
        b = table_ref[i // per_owner, i % per_owner]
        within = b % per_factor
        mine = (b >= 0) & (within // per_holder == member)
        return b // per_factor, within % per_holder, mine

    def begin(i, count):
        source, k, mine = locate(i)
        for f in range(4):

            @pl.when(mine & (source == f))
            def _():
                cols = pl.ds(pl.multiple_of(k * BS, BS), BS)
                slot = jnp.minimum(count, slots - 1)
                pltpu.make_async_copy(sources[f].at[:, cols], held.at[slot], sems.at[slot]).start()

        return count + jnp.where(mine, 1, 0)

    count = lax.fori_loop(0, owners * per_owner, begin, 0)
    for j in range(out_ref.shape[0]):
        if j >= slots:
            out_ref[j] = jnp.zeros(out_ref.shape[1:], jnp.float32)
            continue

        @pl.when(j < count)
        def _():
            pltpu.make_async_copy(sources[0].at[:, pl.ds(0, BS)], held.at[j], sems.at[j]).wait()
            out_ref[j] = held[j].astype(jnp.float32)

        @pl.when(j >= count)
        def _():
            out_ref[j] = jnp.zeros(out_ref.shape[1:], jnp.float32)


def pick(table, sources, per_holder, per_factor, slots, places):
    rows = sources[0].shape[0]
    return pl.pallas_call(
        functools.partial(pick_kernel, per_holder, per_factor, slots),
        out_shape=jax.ShapeDtypeStruct((places, rows, BS), jnp.float32),
        in_specs=[pl.BlockSpec(memory_space=pltpu.SMEM)] + [pl.BlockSpec(memory_space=pl.ANY)] * 4,
        out_specs=pl.BlockSpec(memory_space=pltpu.VMEM),
        scratch_shapes=[
            pltpu.VMEM((slots, rows, BS), jnp.bfloat16),
            pltpu.SemaphoreType.DMA((slots,)),
        ],
        compiler_params=pltpu.CompilerParams(vmem_limit_bytes=48 << 20),
    )(table, *sources)


def exchange_kernel(replicas, span, slots, picked_ref, out_ref, send_sems, recv_sems, own_sem):
    me = lax.axis_index("dp")
    barrier = pltpu.get_barrier_semaphore()

    def greet(d, carry):
        pl.semaphore_signal(
            barrier, inc=1, device_id={"dp": (me + d) % replicas}, device_id_type=pl.DeviceIdType.MESH
        )
        return carry

    lax.fori_loop(1, replicas, greet, 0)
    pl.semaphore_wait(barrier, replicas - 1)

    def copy(d):
        target = (me + d) % replicas
        return target % span < slots, pltpu.make_async_remote_copy(
            src_ref=picked_ref.at[target % span],
            dst_ref=out_ref.at[me],
            send_sem=send_sems.at[d],
            recv_sem=recv_sems.at[d],
            device_id={"dp": target},
            device_id_type=pl.DeviceIdType.MESH,
        )

    def begin(d, carry):
        wanted, moving = copy(d)

        @pl.when(wanted)
        def _():
            moving.start()

        return carry

    lax.fori_loop(1, replicas, begin, 0)
    own = pltpu.make_async_copy(picked_ref.at[me % span], out_ref.at[me], own_sem)
    own.start()
    own.wait()

    def end(d, carry):
        wanted, moving = copy(d)

        @pl.when(wanted)
        def _():
            moving.wait_send()

        @pl.when(me % span < slots)
        def _():
            moving.wait_recv()

        return carry

    lax.fori_loop(1, replicas, end, 0)


def exchange(picked, replicas, span, slots):
    return pl.pallas_call(
        functools.partial(exchange_kernel, replicas, span, slots),
        out_shape=jax.ShapeDtypeStruct((replicas,) + picked.shape[1:], jnp.float32),
        in_specs=[pl.BlockSpec(memory_space=pltpu.VMEM)],
        out_specs=pl.BlockSpec(memory_space=pltpu.VMEM),
        scratch_shapes=[
            pltpu.SemaphoreType.DMA((replicas,)),
            pltpu.SemaphoreType.DMA((replicas,)),
            pltpu.SemaphoreType.DMA,
        ],
        compiler_params=pltpu.CompilerParams(
            collective_id=0, has_side_effects=True, vmem_limit_bytes=48 << 20
        ),
    )(picked)


def place_kernel(per_holder, per_factor, workers, table_ref, bases_ref, out_ref, held, zeros, counts, sems):
    owners, per_owner = table_ref.shape
    flat = owners * per_owner
    for h in range(workers):
        counts[h] = 0

    def begin(i, carry):
        b = table_ref[i // per_owner, i % per_owner]

        @pl.when(b >= 0)
        def _():
            holder = b % per_factor // per_holder
            nth = counts[holder]
            counts[holder] = nth + 1
            pltpu.make_async_copy(
                bases_ref.at[nth * workers + holder], held.at[i], sems.at[0, i]
            ).start()

        return carry

    lax.fori_loop(0, flat, begin, 0)
    zeros[...] = jnp.zeros_like(zeros)

    def empty(i, carry):
        @pl.when(table_ref[i // per_owner, i % per_owner] < 0)
        def _():
            pltpu.make_async_copy(zeros, out_ref.at[i], sems.at[1, i]).start()

        return carry

    lax.fori_loop(0, flat, empty, 0)

    def forward(i, carry):
        @pl.when(table_ref[i // per_owner, i % per_owner] >= 0)
        def _():
            pltpu.make_async_copy(bases_ref.at[0], held.at[i], sems.at[0, i]).wait()
            pltpu.make_async_copy(held.at[i], out_ref.at[i], sems.at[1, i]).start()

        return carry

    lax.fori_loop(0, flat, forward, 0)

    def end(i, carry):
        pltpu.make_async_copy(zeros, out_ref.at[i], sems.at[1, i]).wait()
        return carry

    lax.fori_loop(0, flat, end, 0)


def place(table, bases, per_holder, per_factor, workers):
    flat = table.shape[0] * table.shape[1]
    return pl.pallas_call(
        functools.partial(place_kernel, per_holder, per_factor, workers),
        out_shape=jax.ShapeDtypeStruct((flat, BS, BS), jnp.float32),
        in_specs=[pl.BlockSpec(memory_space=pltpu.SMEM), pl.BlockSpec(memory_space=pl.ANY)],
        out_specs=pl.BlockSpec(memory_space=pl.ANY),
        scratch_shapes=[
            pltpu.VMEM((flat, BS, BS), jnp.float32),
            pltpu.VMEM((BS, BS), jnp.float32),
            pltpu.SMEM((workers,), jnp.int32),
            pltpu.SemaphoreType.DMA((2, flat)),
        ],
        compiler_params=pltpu.CompilerParams(vmem_limit_bytes=48 << 20),
    )(table, bases)


def basis_kernel(x_ref, o_ref, f_ref, q_ref):
    basis_body(x_ref, f_ref, q_ref)
    o_ref[...] = q_ref[ITERS - 1].T * math.sqrt(BS)


def basis(x):
    return pl.pallas_call(
        basis_kernel,
        out_shape=jax.ShapeDtypeStruct((BS, BS), jnp.float32),
        scratch_shapes=[
            pltpu.VMEM((BS, BS), jnp.float32),
            pltpu.VMEM((ITERS, BS, BS), jnp.float32),
        ],
        compiler_params=pltpu.CompilerParams(vmem_limit_bytes=48 << 20),
    )(x)


def per_device(act_one, grad_one, act_two, grad_two, owner_table):
    workers = lax.axis_size("work")
    replicas = lax.axis_size("dp")
    tok_rows, feature_width = act_one.shape
    per_holder = feature_width // BS
    per_factor = per_holder * workers
    slots = owner_table.shape[1]
    span = next(n for n in range(slots, replicas + 1) if replicas % n == 0)
    picked = pick(
        owner_table, (act_one, grad_one, act_two, grad_two), per_holder, per_factor, slots, span
    )
    mine = exchange(picked, replicas, span, slots)
    base = basis(mine.reshape(replicas * tok_rows, BS))
    groups = None
    if span < replicas:
        each = span * workers
        groups = [list(range(i, i + each)) for i in range(0, replicas * workers, each)]
    bases = lax.all_gather(base, ("dp", "work"), axis=0, tiled=False, axis_index_groups=groups)
    placed = place(owner_table, bases, per_holder, per_factor, workers)
    return placed.reshape(workers, slots, BS, BS)


def solution(mesh):
    in_specs = (P("dp", "work"), P("dp", "work"), P("dp", "work"), P("dp", "work"), P())
    return jax.shard_map(
        per_device, mesh=mesh, in_specs=in_specs, out_specs=P(), check_vma=False
    )
```
